32 devices in a mesh: seq: 4 (over z), head: 8 (over y, x, core).
Axes of the slice: x: 2, y: 2, z: 4, core: 2. Of those that a mesh axis runs over, the one named last changes fastest.
Arguments:
- query_raw: bfloat16 [4096, 8192], P('seq', 'head'), may hold values from -12 to 12
- key_raw: bfloat16 [4096, 8192], P('seq', 'head'), may hold values from -6 to 6
- value_raw: bfloat16 [4096, 8192], P('seq', 'head'), may hold values from -6 to 6
- query_gain: float32 [8192], P('head'), may hold values from 0.1 to 1.9
- log_decay: float32 [64, 4096], P('head', 'seq'), may hold values from -1.5 to 0
- out_grad: bfloat16 [4096, 8192], P('seq', 'head'), may hold values from -0.75 to 0.75
Outputs:
- query_raw_grad: bfloat16 [4096, 8192], P(('seq', 'head'))
- key_raw_grad: bfloat16 [4096, 8192], P(('seq', 'head'))
- value_raw_grad: bfloat16 [4096, 8192], P(('seq', 'head'))
The draws below stay inside these ranges and needn't reach their ends.
All inputs are finite; a program needn't handle non-finite values.
Results may differ from the reference program's by a relative error of at most 0.0021.
Values may be sent and summed in bfloat16 or wider, within the bound.
A program may use at most 128 MiB of HBM per device.

```python
import math
import jax
import jax.numpy as jnp
from jax import lax

H = 64
HD = 128
D = 8192
TOKENS = 4096


def draw_query_raw(key, part):
    streams = jax.random.split(jax.random.fold_in(key, 11), 3)
    entries = jax.random.truncated_normal(streams[0], -4.0, 4.0, (TOKENS, D), jnp.float32)
    row_scale = 0.1 * jnp.exp(jax.random.uniform(streams[1], (TOKENS, 1), jnp.float32, 0.0, math.log(10.0)))
    column = lax.broadcasted_iota(jnp.int32, (D,), 0).astype(jnp.float32)
    col_scale = 0.1 * jnp.exp(jax.random.uniform(streams[2], (D,), jnp.float32, 0.0, math.log(10.0)))
    col_scale = col_scale * jnp.exp(math.log(3.0) * column / D)
    return (entries * row_scale * col_scale[None, :]).astype(jnp.bfloat16)


def draw_log_decay(key, part):
    streams = jax.random.split(jax.random.fold_in(key, 23), 4)
    share = 0.5
    quick = jax.random.bernoulli(streams[0], share, (H, 1))
    initial_amount = jnp.where(quick, 1.0 / 40.0, 0.3 / TOKENS)
    multiplier = jnp.exp(jax.random.uniform(streams[1], (H, TOKENS), jnp.float32, -math.log(2.0), math.log(2.0)))
    location_sequence = jax.random.randint(streams[2], (H, 2), 0, TOKENS)
    objective_numbers = jax.random.uniform(streams[3], (H, 2), jnp.float32, 0.2, 0.5)
    element_slot = lax.broadcasted_iota(jnp.int32, (H, 2, TOKENS), 2)
    cluster_sets = jnp.sum(jnp.where(element_slot == location_sequence[:, :, None], jnp.log1p(-objective_numbers)[:, :, None], 0.0), axis=1)
    return -initial_amount * multiplier + cluster_sets


def levels(key, extent, cuts, smallest, largest):
    def one(position, parts):
        steps = jax.random.uniform(jax.random.fold_in(jax.random.fold_in(key, 6), position), (parts,), jnp.float32, smallest / len(cuts), largest / len(cuts))
        return jnp.repeat(jnp.exp(steps), extent[position] // parts).reshape((-1,) + (1,) * (len(extent) - position - 1))

    level = one(*cuts[0])
    for cut in cuts[1:]:
        level = level * one(*cut)
    return level


def centred(key, shape, spread, reach, shards=(), dtype=jnp.bfloat16):
    gain = levels(key, shape, shards, -0.22, 0.18) if shards else 1.0
    result = jax.random.normal(key, shape, jnp.float32) * spread * gain
    return jnp.minimum(jnp.maximum(result, -reach), reach).astype(dtype)


def setup_inputs(seed: int = 0) -> dict:
    seeds = jax.random.split(jax.random.key(seed), 7)
    return {
        "query_raw": draw_query_raw(jax.random.fold_in(seeds[6], 71), 0),
        "key_raw": centred(seeds[1], (TOKENS, D), 1.0, 6.0, ((0, 4), (1, 8))),
        "value_raw": centred(seeds[2], (TOKENS, D), 1.0, 6.0, ((0, 4), (1, 8))),
        "query_gain": jnp.clip(1.0 + 0.18 * jax.random.normal(seeds[3], (D,), jnp.float32), 0.1, 1.9),
        "log_decay": draw_log_decay(jax.random.fold_in(seeds[6], 71), 0),
        "out_grad": centred(seeds[5], (TOKENS, D), 0.05, 0.75, ((0, 4), (1, 8))),
    }


epsilon = 1e-06

def recurrence(queries, keys, values, decay):
    block_len = math.gcd(TOKENS, 32)
    count = TOKENS // block_len

    def token_step(state_matrix, inputs):
        query_vector, key, value, rate = inputs
        recall_score = jnp.einsum('dzt,dz->dt', state_matrix, key)
        update = value - rate[:, None] * recall_score
        state_matrix = rate[:, None, None] * state_matrix + 2.0 * key[:, :, None] * update[:, None, :]
        return (state_matrix, jnp.einsum('dzt,dz->dt', state_matrix, query_vector))

    @jax.checkpoint
    def block_step(state_matrix, block):
        return lax.scan(token_step, state_matrix, block)

    def split(array):
        return array.reshape((count, block_len) + array.shape[1:])
    start = jnp.zeros((H, HD, HD), jnp.float32)
    _, outputs = lax.scan(block_step, start, (split(queries), split(keys), split(values), split(decay)))
    return outputs.reshape(TOKENS, H, HD)

def reference(query_raw, key_raw, value_raw, query_gain, log_decay, out_grad):
    raw_query = query_raw.astype(jnp.float32)
    inv_rms = 1.0 / jnp.sqrt(lax.optimization_barrier(jnp.mean(raw_query * raw_query, axis=1, keepdims=True)) + epsilon)
    normed = raw_query * inv_rms
    scale = HD ** (-0.5)
    queries = (normed * query_gain * scale).reshape(TOKENS, H, HD)
    raw_key = key_raw.astype(jnp.float32).reshape(TOKENS, H, HD)
    key_scale = 1.0 / jnp.sqrt(lax.optimization_barrier(jnp.sum(raw_key * raw_key, axis=2, keepdims=True)) + epsilon)
    keys = raw_key * key_scale
    values = value_raw.astype(jnp.float32).reshape(TOKENS, H, HD)
    decay = jnp.exp(log_decay).T

    def forward(query_part, key_part, value_part):
        return recurrence(query_part, key_part, value_part, decay)
    head_out, pullback = jax.vjp(forward, queries, keys, values)
    query_grad, key_grad, value_grad = pullback(out_grad.astype(jnp.float32).reshape(TOKENS, H, HD))
    scaled = query_grad.reshape(TOKENS, D) * query_gain * scale
    correction = lax.optimization_barrier(jnp.mean(scaled * normed, axis=1, keepdims=True))
    query_raw_grad = (inv_rms * (scaled - normed * correction)).astype(jnp.bfloat16)
    key_raw_grad = key_scale * (key_grad - keys * lax.optimization_barrier(jnp.sum(keys * key_grad, axis=2, keepdims=True)))
    key_raw_grad = key_raw_grad.reshape(TOKENS, D).astype(jnp.bfloat16)
    value_raw_grad = value_grad.reshape(TOKENS, D).astype(jnp.bfloat16)
    return (query_raw_grad, key_raw_grad, value_raw_grad)
```

```python
import math

import jax
import jax.numpy as jnp
from jax import lax
from jax.experimental import pallas as pl
from jax.experimental.pallas import tpu as pltpu
from jax.sharding import PartitionSpec as P

BLOCK = 128
GROUP = 4
VMEM = 48 * 1024 * 1024

epsilon = 1e-06


def parts(x):
    if isinstance(x, tuple):
        return x
    if x.dtype == jnp.bfloat16:
        return (x,)
    high = x.astype(jnp.bfloat16)
    return (high, (x - high.astype(jnp.float32)).astype(jnp.bfloat16))


def prod(a, b, ca=1, cb=0):
    a, b = parts(a), parts(b)
    pairs = [(x, y) for i, x in enumerate(a) for j, y in enumerate(b) if i + j < 2]
    left = pairs[0][0] if len(pairs) == 1 else jnp.concatenate([x for x, _ in pairs], axis=ca)
    right = pairs[0][1] if len(pairs) == 1 else jnp.concatenate([y for _, y in pairs], axis=cb)
    return lax.dot_general(
        left, right, (((ca,), (cb,)), ((), ())), preferred_element_type=jnp.float32
    )


def slots():
    row = lax.broadcasted_iota(jnp.int32, (BLOCK, BLOCK), 0)
    column = lax.broadcasted_iota(jnp.int32, (BLOCK, BLOCK), 1)
    return row, column


def each(function, *lists):
    return [function(*items) for items in zip(*lists)]


def lanes(ref, group):
    return [ref[:, h * BLOCK : (h + 1) * BLOCK] for h in range(group)]


def key_scales(keys):
    row, column = slots()

    def one(key):
        gram = prod(key, key, 1, 1)
        diag = jnp.where(row == column, gram, 0.0)
        return (
            gram,
            lax.rsqrt(jnp.sum(diag, axis=1, keepdims=True) + epsilon),
            lax.rsqrt(jnp.sum(diag, axis=0, keepdims=True) + epsilon),
        )

    return [one(key) for key in keys]


def decays(crow_ref, ccol_ref, group):
    row, column = slots()
    result = []
    for h in range(group):
        crow = crow_ref[h]
        ccol = ccol_ref[0, :, h : h + 1]
        last = crow[:, BLOCK - 1 :]
        weight = jnp.where(
            row >= column, 2.0 * jnp.exp(jnp.where(row >= column, ccol - crow, 0.0)), 0.0
        )
        result.append((weight, jnp.exp(ccol), jnp.exp(last - ccol), jnp.exp(last)))
    return result


def maps_kernel(k_ref, v_ref, crow_ref, ccol_ref, t_ref, w_ref, u_ref, a_ref, b_ref):
    group = crow_ref.shape[0]
    row, column = slots()
    eye = jnp.where(row == column, 1.0, 0.0)
    keys = lanes(k_ref, group)
    values = lanes(v_ref, group)
    scales = key_scales(keys)
    decay = decays(crow_ref, ccol_ref, group)

    def system(scale, dec):
        return jnp.where(row > column, dec[0] * scale[0] * scale[1] * scale[2], 0.0)

    lower = each(system, scales, decay)

    def pick(x, size):
        inside = (row // (2 * size)) == (column // (2 * size))
        across = (row // size) != (column // size)
        return jnp.where(inside & across, x, 0.0)

    inverse = [eye - pick(x, 1) for x in lower]
    size = 2
    while size < BLOCK:
        split = [parts(x) for x in inverse]
        inner = [prod(pick(x, size), s) for x, s in zip(lower, split)]
        inverse = [t - prod(s, y) for t, s, y in zip(inverse, split, inner)]
        size *= 2
    for h in range(group):
        t_ref[h, 0] = inverse[h]
    crows = [crow_ref[h] for h in range(group)]
    weights = [
        prod(t * (jnp.exp(c) * s[2]), k) for t, c, s, k in zip(inverse, crows, scales, keys)
    ]
    initial = each(prod, inverse, values)
    ends = [d[2] * s[1] for d, s in zip(decay, scales)]
    both = [
        prod(k, 2.0 * e * jnp.concatenate([w, u], axis=1), 0, 0)
        for k, e, w, u in zip(keys, ends, weights, initial)
    ]
    for h in range(group):
        w_ref[h, 0] = weights[h]
        u_ref[h, 0] = initial[h]
        a_ref[h, 0] = decay[h][3] * eye - both[h][:, :BLOCK]
        b_ref[h, 0] = both[h][:, BLOCK:]


def chain_kernel(
    q_ref, k_ref, g_ref, crow_ref, ccol_ref, inv_ref, gain_ref, gcol_ref, w_ref, a_ref, b_ref,
    inner_ref, c_ref, pre_ref, map_ref, adj_ref,
):
    group = crow_ref.shape[0]
    row, column = slots()

    @pl.when(pl.program_id(1) == 0)
    def _():
        eye = jnp.where(row == column, 1.0, 0.0)
        for h in range(group):
            map_ref[h, :, :BLOCK] = eye
            map_ref[h, :, BLOCK:] = jnp.zeros((BLOCK, BLOCK), jnp.float32)
            adj_ref[h] = jnp.zeros((BLOCK, BLOCK), jnp.float32)

    queries = lanes(q_ref, group)
    keys = lanes(k_ref, group)
    grads = lanes(g_ref, group)
    gains = lanes(gain_ref, group)
    inv = inv_ref[...]
    scales = key_scales(keys)
    decay = decays(crow_ref, ccol_ref, group)
    mixing = [
        prod(q, k.astype(jnp.float32) * gs, 1, 1) * (d[0] * inv * s[2])
        for q, k, gs, d, s in zip(queries, keys, gains, decay, scales)
    ]
    inner = [prod(m, g, 0, 0) for m, g in zip(mixing, grads)]
    direct = [
        gcol_ref[h] * prod(queries[h], (decay[h][1] * inv) * grads[h].astype(jnp.float32), 0, 0)
        for h in range(group)
    ]
    adjoint = [direct[h] - prod(w_ref[h, 0], inner[h], 0, 0) for h in range(group)]
    for h in range(group):
        before = map_ref[h]
        pre_ref[h, 0] = before
        inner_ref[h, 0] = inner[h]
        c_ref[h, 0] = adjoint[h]
        adj_ref[h] += prod(before[:, :BLOCK], adjoint[h], 0, 0)
        after = prod(a_ref[h, 0], before)
        map_ref[h, :, :BLOCK] = after[:, :BLOCK]
        map_ref[h, :, BLOCK:] = after[:, BLOCK:] + b_ref[h, 0]


def grads_kernel(
    q_ref, k_ref, g_ref, crow_ref, ccol_ref, inv_ref, gain_ref,
    t_ref, w_ref, u_ref, a_ref, c_ref, inner_ref, pre_ref, in_ref, out_ref,
    dq_ref, dk_ref, dv_ref, corr_ref, carry_ref,
):
    group = crow_ref.shape[0]
    heads = range(group)
    row, column = slots()

    @pl.when(pl.program_id(1) == 0)
    def _():
        carry_ref[...] = out_ref[...]

    queries = lanes(q_ref, group)
    keys = lanes(k_ref, group)
    grads = lanes(g_ref, group)
    gains = lanes(gain_ref, group)
    inv = inv_ref[...]
    scales = key_scales(keys)
    decay = decays(crow_ref, ccol_ref, group)
    start = [
        parts(prod(pre_ref[h, 0, :, :BLOCK], in_ref[h]) + pre_ref[h, 0, :, BLOCK:]) for h in heads
    ]
    end = [parts(carry_ref[h]) for h in heads]
    fresh = [parts(u_ref[h, 0] - prod(w_ref[h, 0], start[h])) for h in heads]
    dfresh = [
        inner_ref[h, 0] + (2.0 * decay[h][2] * scales[h][1]) * prod(keys[h], end[h]) for h in heads
    ]
    for h in heads:
        carry_ref[h] = prod(a_ref[h, 0], end[h], 0, 0) + c_ref[h, 0]
    target = [prod(t_ref[h, 0], dfresh[h], 0, 0) for h in heads]
    tparts = [parts(x) for x in target]
    spread = [decay[h][0] * prod(grads[h], fresh[h], 1, 1) for h in heads]
    pairs = [
        jnp.where(row > column, decay[h][0] * prod(tparts[h], fresh[h], 1, 1), 0.0) for h in heads
    ]
    dquery = [
        decay[h][1] * prod(grads[h], start[h], 1, 1) + prod(spread[h] * scales[h][2], keys[h])
        for h in heads
    ]
    dkey = [
        2.0 * decay[h][2] * prod(fresh[h], end[h], 1, 1)
        - decay[h][1] * prod(tparts[h], start[h], 1, 1)
        for h in heads
    ]
    dkey = [
        dkey[h] - prod((pairs[h] + pairs[h].T) * scales[h][2], keys[h]) for h in heads
    ]
    dkey = [
        dkey[h] + gains[h] * prod(spread[h] * inv, queries[h], 0, 0) for h in heads
    ]
    total = jnp.zeros((BLOCK, 1), jnp.float32)
    for h in heads:
        span = slice(h * BLOCK, (h + 1) * BLOCK)
        scaled = dquery[h] * gains[h]
        dq_ref[:, span] = scaled
        total += jnp.sum(scaled * (queries[h].astype(jnp.float32) * inv), axis=1, keepdims=True)
        dv_ref[:, span] = target[h].astype(jnp.bfloat16)
        scale = scales[h][1]
        unit = keys[h].astype(jnp.float32) * scale
        along = jnp.sum(unit * dkey[h], axis=1, keepdims=True)
        dk_ref[:, span] = (scale * (dkey[h] - unit * along)).astype(jnp.bfloat16)
    corr_ref[0] = total


def shift(value, axis, steps):
    count = lax.axis_size(axis)
    first, last = (max(0, -steps), min(count, count - steps))
    return lax.ppermute(value, axis, [(i, i + steps) for i in range(first, last)])


def apply_map(form, matrix, state):
    return jnp.einsum(form, matrix, state, precision=lax.Precision.HIGHEST)


def per_device(query_raw, key_raw, value_raw, query_gain, log_decay, out_grad):
    rows, width = query_raw.shape
    heads = log_decay.shape[0]
    size = width // heads
    blocks = rows // BLOCK
    group = math.gcd(heads, GROUP)
    groups = heads // group
    full = width * lax.axis_size("head")
    f32 = jnp.float32

    raw_query = query_raw.astype(f32)
    squares = lax.psum(jnp.sum(raw_query * raw_query, axis=1), "head")
    inv = lax.rsqrt(squares / full + epsilon)[:, None]
    gain = query_gain * size ** (-0.5)
    gain_row = gain[None, :]
    gain_col = gain.reshape(heads, size, 1)
    cumul = jnp.cumsum(log_decay.reshape(heads, blocks, BLOCK), axis=2).reshape(heads, rows)
    crow = cumul[:, None, :]
    ccol = cumul.reshape(groups, group, rows).transpose(0, 2, 1)

    def specs(order):
        return dict(
            raw=pl.BlockSpec((BLOCK, group * size), lambda g, b: (order(b), g)),
            crow=pl.BlockSpec((group, 1, BLOCK), lambda g, b: (g, 0, order(b))),
            ccol=pl.BlockSpec((1, BLOCK, group), lambda g, b: (g, order(b), 0)),
            inv=pl.BlockSpec((BLOCK, 1), lambda g, b: (order(b), 0)),
            gain=pl.BlockSpec((1, group * size), lambda g, b: (0, g)),
            gcol=pl.BlockSpec((group, size, 1), lambda g, b: (g, 0, 0)),
            mat=pl.BlockSpec((group, 1, size, size), lambda g, b: (g, order(b), 0, 0)),
            pre=pl.BlockSpec((group, 1, size, 2 * size), lambda g, b: (g, order(b), 0, 0)),
            head=pl.BlockSpec((group, size, size), lambda g, b: (g, 0, 0)),
            map=pl.BlockSpec((group, size, 2 * size), lambda g, b: (g, 0, 0)),
            corr=pl.BlockSpec((1, BLOCK, 1), lambda g, b: (g, order(b), 0)),
        )

    grid = (groups, blocks)
    mat = jax.ShapeDtypeStruct((heads, blocks, size, size), f32)
    pre = jax.ShapeDtypeStruct((heads, blocks, size, 2 * size), f32)
    params = pltpu.CompilerParams(
        dimension_semantics=("arbitrary", "arbitrary"), vmem_limit_bytes=VMEM
    )

    def cost(passes):
        flops = 2 * passes * BLOCK**3 * heads * blocks
        return pl.CostEstimate(flops=flops, bytes_accessed=24 * 2**20, transcendentals=0)

    s = specs(lambda b: b)
    inverse, weight, initial, trans, offset = pl.pallas_call(
        maps_kernel,
        grid=grid,
        in_specs=[s["raw"], s["raw"], s["crow"], s["ccol"]],
        out_specs=[s["mat"]] * 5,
        out_shape=[mat] * 5,
        compiler_params=params,
        cost_estimate=cost(160),
        name="block_maps",
    )(key_raw, value_raw, crow, ccol)
    inner, adjoint, prefix, device_map, device_adjoint = pl.pallas_call(
        chain_kernel,
        grid=grid,
        in_specs=[s["raw"]] * 3
        + [s["crow"], s["ccol"], s["inv"], s["gain"], s["gcol"]]
        + [s["mat"]] * 3,
        out_specs=[s["mat"], s["mat"], s["pre"], s["map"], s["head"]],
        out_shape=[
            mat,
            mat,
            pre,
            jax.ShapeDtypeStruct((heads, size, 2 * size), f32),
            jax.ShapeDtypeStruct((heads, size, size), f32),
        ],
        compiler_params=params,
        cost_estimate=cost(80),
        name="device_maps",
    )(
        query_raw, key_raw, out_grad, crow, ccol, inv, gain_row, gain_col, weight, trans, offset
    )

    through, shifted = device_map[:, :, :size], device_map[:, :, size:]
    incoming = jnp.zeros((heads, size, size), f32)
    outgoing = jnp.zeros((heads, size, size), f32)
    for step in range(lax.axis_size("seq") - 1):
        ahead, back = shifted, device_adjoint
        if step:
            ahead = apply_map("hij,hjk->hik", through, incoming) + ahead
            back = apply_map("hji,hjk->hik", through, outgoing) + back
        incoming = shift(ahead, "seq", 1)
        outgoing = shift(back, "seq", -1)

    s = specs(lambda b: blocks - 1 - b)
    scaled, key_grad, value_grad, correction = pl.pallas_call(
        grads_kernel,
        grid=grid,
        in_specs=[s["raw"]] * 3
        + [s["crow"], s["ccol"], s["inv"], s["gain"]]
        + [s["mat"]] * 6
        + [s["pre"], s["head"], s["head"]],
        out_specs=[s["raw"], s["raw"], s["raw"], s["corr"]],
        out_shape=[
            jax.ShapeDtypeStruct((rows, width), f32),
            jax.ShapeDtypeStruct((rows, width), jnp.bfloat16),
            jax.ShapeDtypeStruct((rows, width), jnp.bfloat16),
            jax.ShapeDtypeStruct((groups, rows, 1), f32),
        ],
        scratch_shapes=[pltpu.VMEM((group, size, size), f32)],
        compiler_params=params,
        cost_estimate=cost(160),
        name="block_grads",
    )(
        query_raw, key_raw, out_grad, crow, ccol, inv, gain_row,
        inverse, weight, initial, trans, adjoint, inner, prefix, incoming, outgoing,
    )

    correction = lax.psum(jnp.sum(correction, axis=0), "head") / full
    query_grad = (inv * (scaled - raw_query * inv * correction)).astype(jnp.bfloat16)

    def to_owner(array):
        return lax.all_to_all(array, "head", split_axis=0, concat_axis=1, tiled=True)

    return to_owner(query_grad), to_owner(key_grad), to_owner(value_grad)


def solution(mesh):
    in_specs = (
        P("seq", "head"),
        P("seq", "head"),
        P("seq", "head"),
        P("head"),
        P("head", "seq"),
        P("seq", "head"),
    )
    out_specs = (P(("seq", "head"), None), P(("seq", "head"), None), P(("seq", "head"), None))
    return jax.shard_map(
        per_device, mesh=mesh, in_specs=in_specs, out_specs=out_specs, check_vma=False
    )
```

```python
import functools
import math

import jax
import jax.numpy as jnp
from jax import lax
from jax.experimental import pallas as pl
from jax.experimental.pallas import tpu as pltpu
from jax.sharding import PartitionSpec as P

BLOCK = 128
GROUP = 4
VMEM = 48 * 1024 * 1024

epsilon = 1e-06


def parts(x):
    if isinstance(x, tuple):
        return x
    if x.dtype == jnp.bfloat16:
        return (x,)
    high = x.astype(jnp.bfloat16)
    return (high, (x - high.astype(jnp.float32)).astype(jnp.bfloat16))


def prod(a, b, ca=1, cb=0):
    a, b = parts(a), parts(b)
    pairs = [(x, y) for i, x in enumerate(a) for j, y in enumerate(b) if i + j < 2]
    left = pairs[0][0] if len(pairs) == 1 else jnp.concatenate([x for x, _ in pairs], axis=ca)
    right = pairs[0][1] if len(pairs) == 1 else jnp.concatenate([y for _, y in pairs], axis=cb)
    return lax.dot_general(
        left, right, (((ca,), (cb,)), ((), ())), preferred_element_type=jnp.float32
    )


def slots():
    row = lax.broadcasted_iota(jnp.int32, (BLOCK, BLOCK), 0)
    column = lax.broadcasted_iota(jnp.int32, (BLOCK, BLOCK), 1)
    return row, column


def each(function, *lists):
    return [function(*items) for items in zip(*lists)]


def lanes(ref, group):
    return [ref[:, h * BLOCK : (h + 1) * BLOCK] for h in range(group)]


def key_scales(keys):
    row, column = slots()

    def one(key):
        gram = prod(key, key, 1, 1)
        diag = jnp.where(row == column, gram, 0.0)
        return (
            gram,
            lax.rsqrt(jnp.sum(diag, axis=1, keepdims=True) + epsilon),
            lax.rsqrt(jnp.sum(diag, axis=0, keepdims=True) + epsilon),
        )

    return [one(key) for key in keys]


def decays(crow_ref, ccol_ref, group):
    row, column = slots()
    result = []
    for h in range(group):
        crow = crow_ref[h]
        ccol = ccol_ref[0, :, h : h + 1]
        last = crow[:, BLOCK - 1 :]
        weight = jnp.where(
            row >= column, 2.0 * jnp.exp(jnp.where(row >= column, ccol - crow, 0.0)), 0.0
        )
        result.append((weight, jnp.exp(ccol), jnp.exp(last - ccol), jnp.exp(last)))
    return result


def maps_kernel(k_ref, v_ref, crow_ref, ccol_ref, t_ref, w_ref, u_ref, a_ref, b_ref):
    group = crow_ref.shape[0]
    row, column = slots()
    eye = jnp.where(row == column, 1.0, 0.0)
    keys = lanes(k_ref, group)
    values = lanes(v_ref, group)
    scales = key_scales(keys)
    decay = decays(crow_ref, ccol_ref, group)

    def system(scale, dec):
        return jnp.where(row > column, dec[0] * scale[0] * scale[1] * scale[2], 0.0)

    lower = each(system, scales, decay)

    def pick(x, size):
        inside = (row // (2 * size)) == (column // (2 * size))
        across = (row // size) != (column // size)
        return jnp.where(inside & across, x, 0.0)

    inverse = [eye - pick(x, 1) for x in lower]
    size = 2
    while size < BLOCK:
        split = [parts(x) for x in inverse]
        inner = [prod(pick(x, size), s) for x, s in zip(lower, split)]
        inverse = [t - prod(s, y) for t, s, y in zip(inverse, split, inner)]
        size *= 2
    for h in range(group):
        t_ref[h, 0] = inverse[h]
    crows = [crow_ref[h] for h in range(group)]
    weights = [
        prod(t * (jnp.exp(c) * s[2]), k) for t, c, s, k in zip(inverse, crows, scales, keys)
    ]
    initial = each(prod, inverse, values)
    ends = [d[2] * s[1] for d, s in zip(decay, scales)]
    both = [
        prod(k, 2.0 * e * jnp.concatenate([w, u], axis=1), 0, 0)
        for k, e, w, u in zip(keys, ends, weights, initial)
    ]
    for h in range(group):
        w_ref[h, 0] = weights[h]
        u_ref[h, 0] = initial[h]
        a_ref[h, 0] = decay[h][3] * eye - both[h][:, :BLOCK]
        b_ref[h, 0] = both[h][:, BLOCK:]


def chain_kernel(
    q_ref, k_ref, g_ref, crow_ref, ccol_ref, inv_ref, gain_ref, gcol_ref, w_ref, a_ref, b_ref,
    inner_ref, c_ref, pre_ref, map_ref, adj_ref,
):
    group = crow_ref.shape[0]
    row, column = slots()

    @pl.when(pl.program_id(1) == 0)
    def _():
        eye = jnp.where(row == column, 1.0, 0.0)
        for h in range(group):
            map_ref[h, :, :BLOCK] = eye
            map_ref[h, :, BLOCK:] = jnp.zeros((BLOCK, BLOCK), jnp.float32)
            adj_ref[h] = jnp.zeros((BLOCK, BLOCK), jnp.float32)

    queries = lanes(q_ref, group)
    keys = lanes(k_ref, group)
    grads = lanes(g_ref, group)
    gains = lanes(gain_ref, group)
    inv = inv_ref[...]
    scales = key_scales(keys)
    decay = decays(crow_ref, ccol_ref, group)
    mixing = [
        prod(q, k.astype(jnp.float32) * gs, 1, 1) * (d[0] * inv * s[2])
        for q, k, gs, d, s in zip(queries, keys, gains, decay, scales)
    ]
    inner = [prod(m, g, 0, 0) for m, g in zip(mixing, grads)]
    direct = [
        gcol_ref[h] * prod(queries[h], (decay[h][1] * inv) * grads[h].astype(jnp.float32), 0, 0)
        for h in range(group)
    ]
    adjoint = [direct[h] - prod(w_ref[h, 0], inner[h], 0, 0) for h in range(group)]
    for h in range(group):
        before = map_ref[h]
        pre_ref[h, 0] = before
        inner_ref[h, 0] = inner[h]
        c_ref[h, 0] = adjoint[h]
        adj_ref[h] += prod(before[:, :BLOCK], adjoint[h], 0, 0)
        after = prod(a_ref[h, 0], before)
        map_ref[h, :, :BLOCK] = after[:, :BLOCK]
        map_ref[h, :, BLOCK:] = after[:, BLOCK:] + b_ref[h, 0]


def grads_kernel(
    q_ref, k_ref, g_ref, crow_ref, ccol_ref, inv_ref, gain_ref,
    t_ref, w_ref, u_ref, a_ref, c_ref, inner_ref, pre_ref, in_ref, out_ref,
    dq_ref, dk_ref, dv_ref, corr_ref, carry_ref,
):
    group = crow_ref.shape[0]
    heads = range(group)
    row, column = slots()

    @pl.when(pl.program_id(1) == 0)
    def _():
        carry_ref[...] = out_ref[...]

    queries = lanes(q_ref, group)
    keys = lanes(k_ref, group)
    grads = lanes(g_ref, group)
    gains = lanes(gain_ref, group)
    inv = inv_ref[...]
    scales = key_scales(keys)
    decay = decays(crow_ref, ccol_ref, group)
    start = [
        parts(prod(pre_ref[h, 0, :, :BLOCK], in_ref[h]) + pre_ref[h, 0, :, BLOCK:]) for h in heads
    ]
    end = [parts(carry_ref[h]) for h in heads]
    fresh = [parts(u_ref[h, 0] - prod(w_ref[h, 0], start[h])) for h in heads]
    dfresh = [
        inner_ref[h, 0] + (2.0 * decay[h][2] * scales[h][1]) * prod(keys[h], end[h]) for h in heads
    ]
    for h in heads:
        carry_ref[h] = prod(a_ref[h, 0], end[h], 0, 0) + c_ref[h, 0]
    target = [prod(t_ref[h, 0], dfresh[h], 0, 0) for h in heads]
    tparts = [parts(x) for x in target]
    spread = [decay[h][0] * prod(grads[h], fresh[h], 1, 1) for h in heads]
    pairs = [
        jnp.where(row > column, decay[h][0] * prod(tparts[h], fresh[h], 1, 1), 0.0) for h in heads
    ]
    dquery = [
        decay[h][1] * prod(grads[h], start[h], 1, 1) + prod(spread[h] * scales[h][2], keys[h])
        for h in heads
    ]
    dkey = [
        2.0 * decay[h][2] * prod(fresh[h], end[h], 1, 1)
        - decay[h][1] * prod(tparts[h], start[h], 1, 1)
        for h in heads
    ]
    dkey = [
        dkey[h] - prod((pairs[h] + pairs[h].T) * scales[h][2], keys[h]) for h in heads
    ]
    dkey = [
        dkey[h] + gains[h] * prod(spread[h] * inv, queries[h], 0, 0) for h in heads
    ]
    total = jnp.zeros((BLOCK, 1), jnp.float32)
    for h in heads:
        span = slice(h * BLOCK, (h + 1) * BLOCK)
        scaled = dquery[h] * gains[h]
        dq_ref[:, span] = scaled
        total += jnp.sum(scaled * (queries[h].astype(jnp.float32) * inv), axis=1, keepdims=True)
        dv_ref[:, span] = target[h].astype(jnp.bfloat16)
        scale = scales[h][1]
        unit = keys[h].astype(jnp.float32) * scale
        along = jnp.sum(unit * dkey[h], axis=1, keepdims=True)
        dk_ref[:, span] = (scale * (dkey[h] - unit * along)).astype(jnp.bfloat16)
    corr_ref[0] = total


def greet(axis, count):
    me = lax.axis_index(axis)
    barrier = pltpu.get_barrier_semaphore()
    for offset in range(1, count):
        pl.semaphore_signal(
            barrier,
            inc=1,
            device_id={axis: lax.rem(me + offset, count)},
            device_id_type=pl.DeviceIdType.MESH,
        )
    pl.semaphore_wait(barrier, count - 1)


def remote(source, target, send, receive, axis, index):
    return pltpu.make_async_remote_copy(
        src_ref=source,
        dst_ref=target,
        send_sem=send,
        recv_sem=receive,
        device_id={axis: index},
        device_id_type=pl.DeviceIdType.MESH,
    )


def share_rows(count, mine_ref, held_ref, send, receive):
    me = lax.axis_index("head")
    copies = [
        remote(
            mine_ref, held_ref.at[k], send.at[k], receive.at[k], "head", lax.rem(me + k, count)
        )
        for k in range(1, count)
    ]
    for copy in copies:
        copy.start()
    return copies


def total_kernel(count, mine_ref, total_ref, held_ref, send, receive):
    greet("head", count)
    copies = share_rows(count, mine_ref, held_ref, send, receive)
    for copy in copies:
        copy.wait()
    total = mine_ref[...]
    for k in range(1, count):
        total += held_ref[k]
    total_ref[...] = total


def states_kernel(
    count, map_ref, adj_ref, in_ref, out_ref,
    fsend, frecv, bsend, brecv, fsend_sem, frecv_sem, bsend_sem, brecv_sem,
):
    heads = adj_ref.shape[0]
    me = lax.axis_index("seq")
    first, last = me == 0, me == count - 1
    barrier = pltpu.get_barrier_semaphore()
    before, after = jnp.maximum(me - 1, 0), jnp.minimum(me + 1, count - 1)
    mesh_id = pl.DeviceIdType.MESH

    @pl.when(jnp.logical_not(first))
    def _():
        pl.semaphore_signal(barrier, inc=1, device_id={"seq": before}, device_id_type=mesh_id)

    @pl.when(jnp.logical_not(last))
    def _():
        pl.semaphore_signal(barrier, inc=1, device_id={"seq": after}, device_id_type=mesh_id)

    @pl.when(first | last)
    def _():
        pl.semaphore_wait(barrier, 1)

    @pl.when(jnp.logical_not(first | last))
    def _():
        pl.semaphore_wait(barrier, 2)

    def forward(h):
        return remote(
            fsend.at[h], frecv.at[h], fsend_sem.at[h], frecv_sem.at[h], "seq", after
        )

    def backward(h):
        return remote(
            bsend.at[h], brecv.at[h], bsend_sem.at[h], brecv_sem.at[h], "seq", before
        )

    def run(h, start, end, copy, recv, send, result, step):
        @pl.when(start)
        def _():
            result[h] = jnp.zeros_like(result[h])
            send[h] = step(h, None)

        @pl.when(jnp.logical_not(start))
        def _():
            copy(h).wait_recv()
            result[h] = recv[h]

            @pl.when(jnp.logical_not(end))
            def _():
                send[h] = step(h, recv[h])

        @pl.when(jnp.logical_not(end))
        def _():
            copy(h).start()

    def forward_step(h, state):
        offset = map_ref[h, :, BLOCK:]
        return offset if state is None else prod(map_ref[h, :, :BLOCK], state) + offset

    def backward_step(h, state):
        offset = adj_ref[h]
        return offset if state is None else prod(map_ref[h, :, :BLOCK], state, 0, 0) + offset

    def turn(t, _):
        h = t - me

        @pl.when((h >= 0) & (h < heads))
        def _():
            run(h, first, last, forward, frecv, fsend, in_ref, forward_step)

        k = t - (count - 1 - me)

        @pl.when((k >= 0) & (k < heads))
        def _():
            run(k, last, first, backward, brecv, bsend, out_ref, backward_step)

        return 0

    lax.fori_loop(0, heads + count - 1, turn, 0)

    @pl.when(jnp.logical_not(last))
    def _():
        for h in range(heads):
            forward(h).wait_send()

    @pl.when(jnp.logical_not(first))
    def _():
        for h in range(heads):
            backward(h).wait_send()


def finish_kernel(
    count, full, scaled_hbm, query_hbm, key_hbm, value_hbm, inv_ref, corr_ref,
    dq_hbm, dk_hbm, dv_hbm,
    scaled, query, grad, held, load_sem, corr_send, corr_recv, send, receive, own_sem,
):
    me = lax.axis_index("head")
    rows, width = scaled.shape
    own = rows // count
    blocks = rows // BLOCK
    loads = [
        pltpu.make_async_copy(scaled_hbm, scaled, load_sem.at[0]),
        pltpu.make_async_copy(query_hbm, query, load_sem.at[1]),
    ]
    for load in loads:
        load.start()
    greet("head", count)
    shares = share_rows(count, corr_ref, held, corr_send, corr_recv)
    columns = pl.ds(pl.multiple_of(me * width, width), width)

    def span(index):
        return pl.ds(pl.multiple_of(index * own, own), own)

    def sends(slot, source, target):
        return [
            remote(
                source.at[span(lax.rem(me + k, count))],
                target.at[:, columns],
                send.at[slot, k],
                receive.at[slot, k],
                "head",
                lax.rem(me + k, count),
            )
            for k in range(1, count)
        ]

    def keep(slot, source, target):
        return pltpu.make_async_copy(
            source.at[span(me)], target.at[:, columns], own_sem.at[slot]
        )

    key_sends = sends(1, key_hbm, dk_hbm)
    value_sends = sends(2, value_hbm, dv_hbm)
    query_sends = sends(0, grad, dq_hbm)
    keeps = [keep(1, key_hbm, dk_hbm), keep(2, value_hbm, dv_hbm)]
    for pair in zip(key_sends, value_sends):
        for copy in pair:
            copy.start()
    for copy in keeps:
        copy.start()
    for load in loads:
        load.wait()
    for copy in shares:
        copy.wait()
    total = corr_ref[...]
    for k in range(1, count):
        total += held[k]
    means = (total / full).T
    for b in range(blocks):
        part = slice(b * BLOCK, (b + 1) * BLOCK)
        inv = inv_ref[:, b : b + 1]
        normed = query[part, :].astype(jnp.float32) * inv
        grad[part, :] = (inv * (scaled[part, :] - normed * means[:, b : b + 1])).astype(
            jnp.bfloat16
        )
    last = keep(0, grad, dq_hbm)
    last.start()
    for copy in query_sends:
        copy.start()
    for copy in keeps + [last] + key_sends + value_sends + query_sends:
        copy.wait()


def per_device(query_raw, key_raw, value_raw, query_gain, log_decay, out_grad):
    rows, width = query_raw.shape
    heads = log_decay.shape[0]
    size = width // heads
    blocks = rows // BLOCK
    group = math.gcd(heads, GROUP)
    groups = heads // group
    full = width * lax.axis_size("head")
    f32 = jnp.float32

    raw_query = query_raw.astype(f32)
    count = lax.axis_size("head")
    turns = lax.axis_size("seq")
    dma = pltpu.SemaphoreType.DMA
    in_vmem = pl.BlockSpec(memory_space=pltpu.VMEM)
    anywhere = pl.BlockSpec(memory_space=pl.ANY)
    row_shape = jax.ShapeDtypeStruct((blocks, BLOCK), f32)
    squares = pl.pallas_call(
        functools.partial(total_kernel, count),
        in_specs=[in_vmem],
        out_specs=in_vmem,
        out_shape=row_shape,
        scratch_shapes=[pltpu.VMEM((count, blocks, BLOCK), f32), dma((count,)), dma((count,))],
        compiler_params=pltpu.CompilerParams(collective_id=0, has_side_effects=True),
        name="token_squares",
    )(jnp.sum((raw_query * raw_query).reshape(blocks, BLOCK, width), axis=2))
    inv_rows = lax.rsqrt(squares / full + epsilon)
    inv = inv_rows.reshape(rows, 1)
    gain = query_gain * size ** (-0.5)
    gain_row = gain[None, :]
    gain_col = gain.reshape(heads, size, 1)
    cumul = jnp.cumsum(log_decay.reshape(heads, blocks, BLOCK), axis=2).reshape(heads, rows)
    crow = cumul[:, None, :]
    ccol = cumul.reshape(groups, group, rows).transpose(0, 2, 1)

    def specs(order):
        return dict(
            raw=pl.BlockSpec((BLOCK, group * size), lambda g, b: (order(b), g)),
            crow=pl.BlockSpec((group, 1, BLOCK), lambda g, b: (g, 0, order(b))),
            ccol=pl.BlockSpec((1, BLOCK, group), lambda g, b: (g, order(b), 0)),
            inv=pl.BlockSpec((BLOCK, 1), lambda g, b: (order(b), 0)),
            gain=pl.BlockSpec((1, group * size), lambda g, b: (0, g)),
            gcol=pl.BlockSpec((group, size, 1), lambda g, b: (g, 0, 0)),
            mat=pl.BlockSpec((group, 1, size, size), lambda g, b: (g, order(b), 0, 0)),
            pre=pl.BlockSpec((group, 1, size, 2 * size), lambda g, b: (g, order(b), 0, 0)),
            head=pl.BlockSpec((group, size, size), lambda g, b: (g, 0, 0)),
            map=pl.BlockSpec((group, size, 2 * size), lambda g, b: (g, 0, 0)),
            corr=pl.BlockSpec((1, BLOCK, 1), lambda g, b: (g, order(b), 0)),
        )

    grid = (groups, blocks)
    mat = jax.ShapeDtypeStruct((heads, blocks, size, size), f32)
    pre = jax.ShapeDtypeStruct((heads, blocks, size, 2 * size), f32)
    params = pltpu.CompilerParams(
        dimension_semantics=("arbitrary", "arbitrary"), vmem_limit_bytes=VMEM
    )

    def cost(passes):
        flops = 2 * passes * BLOCK**3 * heads * blocks
        return pl.CostEstimate(flops=flops, bytes_accessed=24 * 2**20, transcendentals=0)

    s = specs(lambda b: b)
    inverse, weight, initial, trans, offset = pl.pallas_call(
        maps_kernel,
        grid=grid,
        in_specs=[s["raw"], s["raw"], s["crow"], s["ccol"]],
        out_specs=[s["mat"]] * 5,
        out_shape=[mat] * 5,
        compiler_params=params,
        cost_estimate=cost(160),
        name="block_maps",
    )(key_raw, value_raw, crow, ccol)
    inner, adjoint, prefix, device_map, device_adjoint = pl.pallas_call(
        chain_kernel,
        grid=grid,
        in_specs=[s["raw"]] * 3
        + [s["crow"], s["ccol"], s["inv"], s["gain"], s["gcol"]]
        + [s["mat"]] * 3,
        out_specs=[s["mat"], s["mat"], s["pre"], s["map"], s["head"]],
        out_shape=[
            mat,
            mat,
            pre,
            jax.ShapeDtypeStruct((heads, size, 2 * size), f32),
            jax.ShapeDtypeStruct((heads, size, size), f32),
        ],
        compiler_params=params,
        cost_estimate=cost(80),
        name="device_maps",
    )(
        query_raw, key_raw, out_grad, crow, ccol, inv, gain_row, gain_col, weight, trans, offset
    )

    state = jax.ShapeDtypeStruct((heads, size, size), f32)
    incoming, outgoing = pl.pallas_call(
        functools.partial(states_kernel, turns),
        in_specs=[in_vmem, in_vmem],
        out_specs=[in_vmem, in_vmem],
        out_shape=[state, state],
        scratch_shapes=[pltpu.VMEM((heads, size, size), f32)] * 4 + [dma((heads,))] * 4,
        compiler_params=pltpu.CompilerParams(
            collective_id=1, has_side_effects=True, vmem_limit_bytes=VMEM
        ),
        name="device_states",
    )(device_map, device_adjoint)

    s = specs(lambda b: blocks - 1 - b)
    scaled, key_grad, value_grad, correction = pl.pallas_call(
        grads_kernel,
        grid=grid,
        in_specs=[s["raw"]] * 3
        + [s["crow"], s["ccol"], s["inv"], s["gain"]]
        + [s["mat"]] * 6
        + [s["pre"], s["head"], s["head"]],
        out_specs=[s["raw"], s["raw"], s["raw"], s["corr"]],
        out_shape=[
            jax.ShapeDtypeStruct((rows, width), f32),
            jax.ShapeDtypeStruct((rows, width), jnp.bfloat16),
            jax.ShapeDtypeStruct((rows, width), jnp.bfloat16),
            jax.ShapeDtypeStruct((groups, rows, 1), f32),
        ],
        scratch_shapes=[pltpu.VMEM((group, size, size), f32)],
        compiler_params=params,
        cost_estimate=cost(160),
        name="block_grads",
    )(
        query_raw, key_raw, out_grad, crow, ccol, inv, gain_row,
        inverse, weight, initial, trans, adjoint, inner, prefix, incoming, outgoing,
    )

    owned = jax.ShapeDtypeStruct((rows // count, full), jnp.bfloat16)
    return pl.pallas_call(
        functools.partial(finish_kernel, count, full),
        in_specs=[anywhere] * 4 + [in_vmem] * 2,
        out_specs=[anywhere] * 3,
        out_shape=[owned] * 3,
        scratch_shapes=[
            pltpu.VMEM((rows, width), f32),
            pltpu.VMEM((rows, width), jnp.bfloat16),
            pltpu.VMEM((rows, width), jnp.bfloat16),
            pltpu.VMEM((count, blocks, BLOCK), f32),
            dma((2,)),
            dma((count,)),
            dma((count,)),
            dma((3, count)),
            dma((3, count)),
            dma((3,)),
        ],
        compiler_params=pltpu.CompilerParams(
            collective_id=2, has_side_effects=True, vmem_limit_bytes=VMEM
        ),
        name="send_gradients",
    )(
        scaled, query_raw, key_grad, value_grad, inv_rows.T,
        jnp.sum(correction, axis=0).reshape(blocks, BLOCK),
    )


def solution(mesh):
    in_specs = (
        P("seq", "head"),
        P("seq", "head"),
        P("seq", "head"),
        P("head"),
        P("head", "seq"),
        P("seq", "head"),
    )
    out_specs = (P(("seq", "head"), None), P(("seq", "head"), None), P(("seq", "head"), None))
    return jax.shard_map(
        per_device, mesh=mesh, in_specs=in_specs, out_specs=out_specs, check_vma=False
    )
```

```python
import functools
import math

import jax
import jax.numpy as jnp
from jax import lax
from jax.experimental import pallas as pl
from jax.experimental.pallas import tpu as pltpu
from jax.sharding import PartitionSpec as P

BLOCK = 128
WIDE = 8
GROUP = 4
VMEM = 48 * 1024 * 1024

epsilon = 1e-06


def parts(x):
    if isinstance(x, tuple):
        return x
    if x.dtype == jnp.bfloat16:
        return (x,)
    high = x.astype(jnp.bfloat16)
    return (high, (x - high.astype(jnp.float32)).astype(jnp.bfloat16))


def prod(a, b, ca=1, cb=0):
    a, b = parts(a), parts(b)
    pairs = [(x, y) for i, x in enumerate(a) for j, y in enumerate(b) if i + j < 2]
    left = pairs[0][0] if len(pairs) == 1 else jnp.concatenate([x for x, _ in pairs], axis=ca)
    right = pairs[0][1] if len(pairs) == 1 else jnp.concatenate([y for _, y in pairs], axis=cb)
    return lax.dot_general(
        left, right, (((ca,), (cb,)), ((), ())), preferred_element_type=jnp.float32
    )


def slots():
    row = lax.broadcasted_iota(jnp.int32, (BLOCK, BLOCK), 0)
    column = lax.broadcasted_iota(jnp.int32, (BLOCK, BLOCK), 1)
    return row, column


def each(function, *lists):
    return [function(*items) for items in zip(*lists)]


def lanes(ref, group):
    return [ref[:, h * BLOCK : (h + 1) * BLOCK] for h in range(group)]


def key_scales(keys):
    row, column = slots()

    def one(key):
        gram = prod(key, key, 1, 1)
        diag = jnp.where(row == column, gram, 0.0)
        return (
            gram,
            lax.rsqrt(jnp.sum(diag, axis=1, keepdims=True) + epsilon),
            lax.rsqrt(jnp.sum(diag, axis=0, keepdims=True) + epsilon),
        )

    return [one(key) for key in keys]


def decays(crow_ref, ccol_ref, group):
    row, column = slots()
    result = []
    for h in range(group):
        crow = crow_ref[h]
        ccol = ccol_ref[0, :, h : h + 1]
        last = crow[:, BLOCK - 1 :]
        weight = jnp.where(
            row >= column, 2.0 * jnp.exp(jnp.where(row >= column, ccol - crow, 0.0)), 0.0
        )
        result.append((weight, jnp.exp(ccol), jnp.exp(last - ccol), jnp.exp(last)))
    return result


def maps_kernel(k_ref, v_ref, crow_ref, ccol_ref, t_ref, w_ref, u_ref, a_ref, b_ref):
    group = crow_ref.shape[0]
    row, column = slots()
    eye = jnp.where(row == column, 1.0, 0.0)
    keys = lanes(k_ref, group)
    values = lanes(v_ref, group)
    scales = key_scales(keys)
    decay = decays(crow_ref, ccol_ref, group)

    def system(scale, dec):
        return jnp.where(row > column, dec[0] * scale[0] * scale[1] * scale[2], 0.0)

    lower = each(system, scales, decay)

    def pick(x, size):
        inside = (row // (2 * size)) == (column // (2 * size))
        across = (row // size) != (column // size)
        return jnp.where(inside & across, x, 0.0)

    def second(x, size):
        return jnp.concatenate(
            [x[i + size : i + 2 * size] for i in range(0, BLOCK, 2 * size)], axis=0
        )

    def spread(x, size):
        zeros = jnp.zeros((size, BLOCK), x.dtype)
        pieces = []
        for i in range(0, BLOCK // 2, size):
            pieces += [zeros, x[i : i + size]]
        return jnp.concatenate(pieces, axis=0)

    inverse = [eye - pick(x, 1) for x in lower]
    size = 2
    while size < BLOCK:
        split = [parts(x) for x in inverse]
        if size < 8:
            inner = [prod(pick(x, size), p) for x, p in zip(lower, split)]
            inverse = [t - prod(p, y) for t, p, y in zip(inverse, split, inner)]
        else:
            inner = [prod(second(pick(x, size), size), p) for x, p in zip(lower, split)]
            change = [prod(second(t, size), spread(y, size)) for t, y in zip(inverse, inner)]
            inverse = [t - spread(y, size) for t, y in zip(inverse, change)]
        size *= 2
    for h in range(group):
        t_ref[h, 0] = inverse[h]
    crows = [crow_ref[h] for h in range(group)]
    weights = [
        prod(t * (jnp.exp(c) * s[2]), k) for t, c, s, k in zip(inverse, crows, scales, keys)
    ]
    initial = each(prod, inverse, values)
    ends = [d[2] * s[1] for d, s in zip(decay, scales)]
    both = [
        prod(k, 2.0 * e * jnp.concatenate([w, u], axis=1), 0, 0)
        for k, e, w, u in zip(keys, ends, weights, initial)
    ]
    for h in range(group):
        w_ref[h, 0] = weights[h]
        u_ref[h, 0] = initial[h]
        a_ref[h, 0] = decay[h][3] * eye - both[h][:, :BLOCK]
        b_ref[h, 0] = both[h][:, BLOCK:]


def chain_kernel(
    q_ref, k_ref, g_ref, crow_ref, ccol_ref, inv_ref, gain_ref, gcol_ref, w_ref, a_ref, b_ref,
    inner_ref, c_ref, pre_ref, map_ref, adj_ref,
):
    group = crow_ref.shape[0]
    row, column = slots()

    @pl.when(pl.program_id(1) == 0)
    def _():
        eye = jnp.where(row == column, 1.0, 0.0)
        for h in range(group):
            map_ref[h, :, :BLOCK] = eye
            map_ref[h, :, BLOCK:] = jnp.zeros((BLOCK, BLOCK), jnp.float32)
            adj_ref[h] = jnp.zeros((BLOCK, BLOCK), jnp.float32)

    queries = lanes(q_ref, group)
    keys = lanes(k_ref, group)
    grads = lanes(g_ref, group)
    gains = lanes(gain_ref, group)
    inv = inv_ref[...]
    scales = key_scales(keys)
    decay = decays(crow_ref, ccol_ref, group)
    mixing = [
        prod(q, k.astype(jnp.float32) * gs, 1, 1) * (d[0] * inv * s[2])
        for q, k, gs, d, s in zip(queries, keys, gains, decay, scales)
    ]
    inner = [prod(m, g, 0, 0) for m, g in zip(mixing, grads)]
    direct = [
        gcol_ref[h] * prod(queries[h], (decay[h][1] * inv) * grads[h].astype(jnp.float32), 0, 0)
        for h in range(group)
    ]
    adjoint = [direct[h] - prod(w_ref[h, 0], inner[h], 0, 0) for h in range(group)]
    for h in range(group):
        before = map_ref[h]
        pre_ref[h, 0] = before
        inner_ref[h, 0] = inner[h]
        c_ref[h, 0] = adjoint[h]
        adj_ref[h] += prod(before[:, :BLOCK], adjoint[h], 0, 0)
        after = prod(a_ref[h, 0], before)
        map_ref[h, :, :BLOCK] = after[:, :BLOCK]
        map_ref[h, :, BLOCK:] = after[:, BLOCK:] + b_ref[h, 0]


def grads_kernel(
    q_ref, k_ref, g_ref, crow_ref, ccol_ref, inv_ref, gain_ref,
    t_ref, w_ref, u_ref, a_ref, c_ref, inner_ref, pre_ref, in_ref, out_ref,
    dq_ref, dk_ref, dv_ref, corr_ref, carry_ref,
):
    group = crow_ref.shape[0]
    heads = range(group)
    row, column = slots()

    @pl.when(pl.program_id(1) == 0)
    def _():
        carry_ref[...] = out_ref[...]

    queries = lanes(q_ref, group)
    keys = lanes(k_ref, group)
    grads = lanes(g_ref, group)
    gains = lanes(gain_ref, group)
    inv = inv_ref[...]
    scales = key_scales(keys)
    decay = decays(crow_ref, ccol_ref, group)
    start = [
        parts(prod(pre_ref[h, 0, :, :BLOCK], in_ref[h]) + pre_ref[h, 0, :, BLOCK:]) for h in heads
    ]
    end = [parts(carry_ref[h]) for h in heads]
    fresh = [parts(u_ref[h, 0] - prod(w_ref[h, 0], start[h])) for h in heads]
    dfresh = [
        inner_ref[h, 0] + (2.0 * decay[h][2] * scales[h][1]) * prod(keys[h], end[h]) for h in heads
    ]
    for h in heads:
        carry_ref[h] = prod(a_ref[h, 0], end[h], 0, 0) + c_ref[h, 0]
    target = [prod(t_ref[h, 0], dfresh[h], 0, 0) for h in heads]
    tparts = [parts(x) for x in target]
    spread = [decay[h][0] * prod(grads[h], fresh[h], 1, 1) for h in heads]
    pairs = [
        jnp.where(row > column, decay[h][0] * prod(tparts[h], fresh[h], 1, 1), 0.0) for h in heads
    ]
    dquery = [
        decay[h][1] * prod(grads[h], start[h], 1, 1) + prod(spread[h] * scales[h][2], keys[h])
        for h in heads
    ]
    dkey = [
        2.0 * decay[h][2] * prod(fresh[h], end[h], 1, 1)
        - decay[h][1] * prod(tparts[h], start[h], 1, 1)
        for h in heads
    ]
    dkey = [
        dkey[h] - prod((pairs[h] + pairs[h].T) * scales[h][2], keys[h]) for h in heads
    ]
    dkey = [
        dkey[h] + gains[h] * prod(spread[h] * inv, queries[h], 0, 0) for h in heads
    ]
    total = jnp.zeros((BLOCK, 1), jnp.float32)
    for h in heads:
        span = slice(h * BLOCK, (h + 1) * BLOCK)
        scaled = dquery[h] * gains[h]
        dq_ref[:, span] = scaled
        total += jnp.sum(scaled * (queries[h].astype(jnp.float32) * inv), axis=1, keepdims=True)
        dv_ref[:, span] = target[h].astype(jnp.bfloat16)
        scale = scales[h][1]
        unit = keys[h].astype(jnp.float32) * scale
        along = jnp.sum(unit * dkey[h], axis=1, keepdims=True)
        dk_ref[:, span] = (scale * (dkey[h] - unit * along)).astype(jnp.bfloat16)
    corr_ref[0] = total


def greet(axis, count):
    me = lax.axis_index(axis)
    barrier = pltpu.get_barrier_semaphore()
    for offset in range(1, count):
        pl.semaphore_signal(
            barrier,
            inc=1,
            device_id={axis: lax.rem(me + offset, count)},
            device_id_type=pl.DeviceIdType.MESH,
        )
    pl.semaphore_wait(barrier, count - 1)


def remote(source, target, send, receive, axis, index):
    return pltpu.make_async_remote_copy(
        src_ref=source,
        dst_ref=target,
        send_sem=send,
        recv_sem=receive,
        device_id={axis: index},
        device_id_type=pl.DeviceIdType.MESH,
    )


def share_rows(count, mine_ref, held_ref, send, receive):
    me = lax.axis_index("head")
    copies = [
        remote(
            mine_ref, held_ref.at[k], send.at[k], receive.at[k], "head", lax.rem(me + k, count)
        )
        for k in range(1, count)
    ]
    for copy in copies:
        copy.start()
    return copies


def total_kernel(count, mine_ref, total_ref, held_ref, send, receive):
    greet("head", count)
    copies = share_rows(count, mine_ref, held_ref, send, receive)
    for copy in copies:
        copy.wait()
    total = mine_ref[...]
    for k in range(1, count):
        total += held_ref[k]
    total_ref[...] = total


def states_kernel(
    count, map_ref, adj_ref, in_ref, out_ref,
    fsend, frecv, bsend, brecv, fsend_sem, frecv_sem, bsend_sem, brecv_sem,
):
    heads = adj_ref.shape[0]
    me = lax.axis_index("seq")
    first, last = me == 0, me == count - 1
    barrier = pltpu.get_barrier_semaphore()
    before, after = jnp.maximum(me - 1, 0), jnp.minimum(me + 1, count - 1)
    mesh_id = pl.DeviceIdType.MESH

    @pl.when(jnp.logical_not(first))
    def _():
        pl.semaphore_signal(barrier, inc=1, device_id={"seq": before}, device_id_type=mesh_id)

    @pl.when(jnp.logical_not(last))
    def _():
        pl.semaphore_signal(barrier, inc=1, device_id={"seq": after}, device_id_type=mesh_id)

    @pl.when(first | last)
    def _():
        pl.semaphore_wait(barrier, 1)

    @pl.when(jnp.logical_not(first | last))
    def _():
        pl.semaphore_wait(barrier, 2)

    def forward(h):
        return remote(
            fsend.at[h], frecv.at[h], fsend_sem.at[h], frecv_sem.at[h], "seq", after
        )

    def backward(h):
        return remote(
            bsend.at[h], brecv.at[h], bsend_sem.at[h], brecv_sem.at[h], "seq", before
        )

    def run(h, start, end, copy, recv, send, result, step):
        @pl.when(start)
        def _():
            result[h] = jnp.zeros_like(result[h])
            send[h] = step(h, None)

        @pl.when(jnp.logical_not(start))
        def _():
            copy(h).wait_recv()
            result[h] = recv[h]

            @pl.when(jnp.logical_not(end))
            def _():
                send[h] = step(h, recv[h])

        @pl.when(jnp.logical_not(end))
        def _():
            copy(h).start()

    def forward_step(h, state):
        offset = map_ref[h, :, BLOCK:]
        return offset if state is None else prod(map_ref[h, :, :BLOCK], state) + offset

    def backward_step(h, state):
        offset = adj_ref[h]
        return offset if state is None else prod(map_ref[h, :, :BLOCK], state, 0, 0) + offset

    def turn(t, _):
        h = t - me

        @pl.when((h >= 0) & (h < heads))
        def _():
            run(h, first, last, forward, frecv, fsend, in_ref, forward_step)

        k = t - (count - 1 - me)

        @pl.when((k >= 0) & (k < heads))
        def _():
            run(k, last, first, backward, brecv, bsend, out_ref, backward_step)

        return 0

    lax.fori_loop(0, heads + count - 1, turn, 0)

    @pl.when(jnp.logical_not(last))
    def _():
        for h in range(heads):
            forward(h).wait_send()

    @pl.when(jnp.logical_not(first))
    def _():
        for h in range(heads):
            backward(h).wait_send()


def finish_kernel(
    count, full, scaled_hbm, query_hbm, key_hbm, value_hbm, inv_ref, corr_ref,
    dq_hbm, dk_hbm, dv_hbm,
    scaled, query, grad, held, load_sem, corr_send, corr_recv, send, receive, own_sem,
):
    me = lax.axis_index("head")
    rows, width = scaled.shape
    own = rows // count
    blocks = rows // BLOCK
    loads = [
        pltpu.make_async_copy(scaled_hbm, scaled, load_sem.at[0]),
        pltpu.make_async_copy(query_hbm, query, load_sem.at[1]),
    ]
    for load in loads:
        load.start()
    greet("head", count)
    shares = share_rows(count, corr_ref, held, corr_send, corr_recv)
    columns = pl.ds(pl.multiple_of(me * width, width), width)

    def span(index):
        return pl.ds(pl.multiple_of(index * own, own), own)

    def sends(slot, source, target):
        return [
            remote(
                source.at[span(lax.rem(me + k, count))],
                target.at[:, columns],
                send.at[slot, k],
                receive.at[slot, k],
                "head",
                lax.rem(me + k, count),
            )
            for k in range(1, count)
        ]

    def keep(slot, source, target):
        return pltpu.make_async_copy(
            source.at[span(me)], target.at[:, columns], own_sem.at[slot]
        )

    key_sends = sends(1, key_hbm, dk_hbm)
    value_sends = sends(2, value_hbm, dv_hbm)
    query_sends = sends(0, grad, dq_hbm)
    keeps = [keep(1, key_hbm, dk_hbm), keep(2, value_hbm, dv_hbm)]
    for pair in zip(key_sends, value_sends):
        for copy in pair:
            copy.start()
    for copy in keeps:
        copy.start()
    for load in loads:
        load.wait()
    for copy in shares:
        copy.wait()
    total = corr_ref[...]
    for k in range(1, count):
        total += held[k]
    means = (total / full).T
    for b in range(blocks):
        part = slice(b * BLOCK, (b + 1) * BLOCK)
        inv = inv_ref[:, b : b + 1]
        normed = query[part, :].astype(jnp.float32) * inv
        grad[part, :] = (inv * (scaled[part, :] - normed * means[:, b : b + 1])).astype(
            jnp.bfloat16
        )
    last = keep(0, grad, dq_hbm)
    last.start()
    for copy in query_sends:
        copy.start()
    for copy in keeps + [last] + key_sends + value_sends + query_sends:
        copy.wait()


def per_device(query_raw, key_raw, value_raw, query_gain, log_decay, out_grad):
    rows, width = query_raw.shape
    heads = log_decay.shape[0]
    size = width // heads
    blocks = rows // BLOCK
    full = width * lax.axis_size("head")
    f32 = jnp.float32

    raw_query = query_raw.astype(f32)
    count = lax.axis_size("head")
    turns = lax.axis_size("seq")
    dma = pltpu.SemaphoreType.DMA
    in_vmem = pl.BlockSpec(memory_space=pltpu.VMEM)
    anywhere = pl.BlockSpec(memory_space=pl.ANY)
    row_shape = jax.ShapeDtypeStruct((blocks, BLOCK), f32)
    squares = pl.pallas_call(
        functools.partial(total_kernel, count),
        in_specs=[in_vmem],
        out_specs=in_vmem,
        out_shape=row_shape,
        scratch_shapes=[pltpu.VMEM((count, blocks, BLOCK), f32), dma((count,)), dma((count,))],
        compiler_params=pltpu.CompilerParams(collective_id=0, has_side_effects=True),
        name="token_squares",
    )(jnp.sum((raw_query * raw_query).reshape(blocks, BLOCK, width), axis=2))
    inv_rows = lax.rsqrt(squares / full + epsilon)
    inv = inv_rows.reshape(rows, 1)
    gain = query_gain * size ** (-0.5)
    gain_row = gain[None, :]
    gain_col = gain.reshape(heads, size, 1)
    cumul = jnp.cumsum(log_decay.reshape(heads, blocks, BLOCK), axis=2).reshape(heads, rows)
    crow = cumul[:, None, :]

    def columns_of(group):
        return cumul.reshape(heads // group, group, rows).transpose(0, 2, 1)

    def specs(group, order):
        return dict(
            raw=pl.BlockSpec((BLOCK, group * size), lambda g, b: (order(b), g)),
            crow=pl.BlockSpec((group, 1, BLOCK), lambda g, b: (g, 0, order(b))),
            ccol=pl.BlockSpec((1, BLOCK, group), lambda g, b: (g, order(b), 0)),
            inv=pl.BlockSpec((BLOCK, 1), lambda g, b: (order(b), 0)),
            gain=pl.BlockSpec((1, group * size), lambda g, b: (0, g)),
            gcol=pl.BlockSpec((group, size, 1), lambda g, b: (g, 0, 0)),
            mat=pl.BlockSpec((group, 1, size, size), lambda g, b: (g, order(b), 0, 0)),
            pre=pl.BlockSpec((group, 1, size, 2 * size), lambda g, b: (g, order(b), 0, 0)),
            head=pl.BlockSpec((group, size, size), lambda g, b: (g, 0, 0)),
            map=pl.BlockSpec((group, size, 2 * size), lambda g, b: (g, 0, 0)),
            corr=pl.BlockSpec((1, BLOCK, 1), lambda g, b: (g, order(b), 0)),
        )

    mat = jax.ShapeDtypeStruct((heads, blocks, size, size), f32)
    pre = jax.ShapeDtypeStruct((heads, blocks, size, 2 * size), f32)
    params = pltpu.CompilerParams(
        dimension_semantics=("arbitrary", "arbitrary"), vmem_limit_bytes=VMEM
    )

    def cost(passes):
        flops = 2 * passes * BLOCK**3 * heads * blocks
        return pl.CostEstimate(flops=flops, bytes_accessed=24 * 2**20, transcendentals=0)

    group = math.gcd(heads, WIDE)
    grid = (heads // group, blocks)
    ccol = columns_of(group)
    s = specs(group, lambda b: b)
    inverse, weight, initial, trans, offset = pl.pallas_call(
        maps_kernel,
        grid=grid,
        in_specs=[s["raw"], s["raw"], s["crow"], s["ccol"]],
        out_specs=[s["mat"]] * 5,
        out_shape=[mat] * 5,
        compiler_params=params,
        cost_estimate=cost(160),
        name="block_maps",
    )(key_raw, value_raw, crow, ccol)
    inner, adjoint, prefix, device_map, device_adjoint = pl.pallas_call(
        chain_kernel,
        grid=grid,
        in_specs=[s["raw"]] * 3
        + [s["crow"], s["ccol"], s["inv"], s["gain"], s["gcol"]]
        + [s["mat"]] * 3,
        out_specs=[s["mat"], s["mat"], s["pre"], s["map"], s["head"]],
        out_shape=[
            mat,
            mat,
            pre,
            jax.ShapeDtypeStruct((heads, size, 2 * size), f32),
            jax.ShapeDtypeStruct((heads, size, size), f32),
        ],
        compiler_params=params,
        cost_estimate=cost(80),
        name="device_maps",
    )(
        query_raw, key_raw, out_grad, crow, ccol, inv, gain_row, gain_col, weight, trans, offset
    )

    state = jax.ShapeDtypeStruct((heads, size, size), f32)
    incoming, outgoing = pl.pallas_call(
        functools.partial(states_kernel, turns),
        in_specs=[in_vmem, in_vmem],
        out_specs=[in_vmem, in_vmem],
        out_shape=[state, state],
        scratch_shapes=[pltpu.VMEM((heads, size, size), f32)] * 4 + [dma((heads,))] * 4,
        compiler_params=pltpu.CompilerParams(
            collective_id=1, has_side_effects=True, vmem_limit_bytes=VMEM
        ),
        name="device_states",
    )(device_map, device_adjoint)

    group = math.gcd(heads, GROUP)
    groups = heads // group
    grid = (groups, blocks)
    ccol = columns_of(group)
    s = specs(group, lambda b: blocks - 1 - b)
    scaled, key_grad, value_grad, correction = pl.pallas_call(
        grads_kernel,
        grid=grid,
        in_specs=[s["raw"]] * 3
        + [s["crow"], s["ccol"], s["inv"], s["gain"]]
        + [s["mat"]] * 6
        + [s["pre"], s["head"], s["head"]],
        out_specs=[s["raw"], s["raw"], s["raw"], s["corr"]],
        out_shape=[
            jax.ShapeDtypeStruct((rows, width), f32),
            jax.ShapeDtypeStruct((rows, width), jnp.bfloat16),
            jax.ShapeDtypeStruct((rows, width), jnp.bfloat16),
            jax.ShapeDtypeStruct((groups, rows, 1), f32),
        ],
        scratch_shapes=[pltpu.VMEM((group, size, size), f32)],
        compiler_params=params,
        cost_estimate=cost(160),
        name="block_grads",
    )(
        query_raw, key_raw, out_grad, crow, ccol, inv, gain_row,
        inverse, weight, initial, trans, adjoint, inner, prefix, incoming, outgoing,
    )

    owned = jax.ShapeDtypeStruct((rows // count, full), jnp.bfloat16)
    return pl.pallas_call(
        functools.partial(finish_kernel, count, full),
        in_specs=[anywhere] * 4 + [in_vmem] * 2,
        out_specs=[anywhere] * 3,
        out_shape=[owned] * 3,
        scratch_shapes=[
            pltpu.VMEM((rows, width), f32),
            pltpu.VMEM((rows, width), jnp.bfloat16),
            pltpu.VMEM((rows, width), jnp.bfloat16),
            pltpu.VMEM((count, blocks, BLOCK), f32),
            dma((2,)),
            dma((count,)),
            dma((count,)),
            dma((3, count)),
            dma((3, count)),
            dma((3,)),
        ],
        compiler_params=pltpu.CompilerParams(
            collective_id=2, has_side_effects=True, vmem_limit_bytes=VMEM
        ),
        name="send_gradients",
    )(
        scaled, query_raw, key_grad, value_grad, inv_rows.T,
        jnp.sum(correction, axis=0).reshape(blocks, BLOCK),
    )


def solution(mesh):
    in_specs = (
        P("seq", "head"),
        P("seq", "head"),
        P("seq", "head"),
        P("head"),
        P("head", "seq"),
        P("seq", "head"),
    )
    out_specs = (P(("seq", "head"), None), P(("seq", "head"), None), P(("seq", "head"), None))
    return jax.shard_map(
        per_device, mesh=mesh, in_specs=in_specs, out_specs=out_specs, check_vma=False
    )
```

```python
import functools
import math

import jax
import jax.numpy as jnp
from jax import lax
from jax.experimental import pallas as pl
from jax.experimental.pallas import tpu as pltpu
from jax.sharding import PartitionSpec as P

BLOCK = 128
WIDE = 8
GROUP = 4
VMEM = 48 * 1024 * 1024

epsilon = 1e-06


def parts(x):
    if isinstance(x, tuple):
        return x
    if x.dtype == jnp.bfloat16:
        return (x,)
    high = x.astype(jnp.bfloat16)
    return (high, (x - high.astype(jnp.float32)).astype(jnp.bfloat16))


def prod(a, b, ca=1, cb=0):
    a, b = parts(a), parts(b)
    pairs = [(x, y) for i, x in enumerate(a) for j, y in enumerate(b) if i + j < 2]
    left = pairs[0][0] if len(pairs) == 1 else jnp.concatenate([x for x, _ in pairs], axis=ca)
    right = pairs[0][1] if len(pairs) == 1 else jnp.concatenate([y for _, y in pairs], axis=cb)
    return lax.dot_general(
        left, right, (((ca,), (cb,)), ((), ())), preferred_element_type=jnp.float32
    )


def slots():
    row = lax.broadcasted_iota(jnp.int32, (BLOCK, BLOCK), 0)
    column = lax.broadcasted_iota(jnp.int32, (BLOCK, BLOCK), 1)
    return row, column


def each(function, *lists):
    return [function(*items) for items in zip(*lists)]


def lanes(ref, group):
    return [ref[:, h * BLOCK : (h + 1) * BLOCK] for h in range(group)]


def key_scales(keys):
    row, column = slots()

    def one(key):
        gram = prod(key, key, 1, 1)
        diag = jnp.where(row == column, gram, 0.0)
        return (
            gram,
            lax.rsqrt(jnp.sum(diag, axis=1, keepdims=True) + epsilon),
            lax.rsqrt(jnp.sum(diag, axis=0, keepdims=True) + epsilon),
        )

    return [one(key) for key in keys]


def decays(crow_ref, ccol_ref, group):
    row, column = slots()
    result = []
    for h in range(group):
        crow = crow_ref[h]
        ccol = ccol_ref[0, :, h : h + 1]
        last = crow[:, BLOCK - 1 :]
        weight = jnp.where(
            row >= column, 2.0 * jnp.exp(jnp.where(row >= column, ccol - crow, 0.0)), 0.0
        )
        result.append((weight, jnp.exp(ccol), jnp.exp(last - ccol), jnp.exp(last)))
    return result


def maps_kernel(k_ref, v_ref, crow_ref, ccol_ref, t_ref, w_ref, u_ref, a_ref, b_ref):
    group = crow_ref.shape[0]
    row, column = slots()
    eye = jnp.where(row == column, 1.0, 0.0)
    keys = lanes(k_ref, group)
    values = lanes(v_ref, group)
    scales = key_scales(keys)
    decay = decays(crow_ref, ccol_ref, group)

    def system(scale, dec):
        return jnp.where(row > column, dec[0] * scale[0] * scale[1] * scale[2], 0.0)

    lower = each(system, scales, decay)

    def pick(x, size):
        inside = (row // (2 * size)) == (column // (2 * size))
        across = (row // size) != (column // size)
        return jnp.where(inside & across, x, 0.0)

    def second(x, size):
        return jnp.concatenate(
            [x[i + size : i + 2 * size] for i in range(0, BLOCK, 2 * size)], axis=0
        )

    def spread(x, size):
        zeros = jnp.zeros((size, BLOCK), x.dtype)
        pieces = []
        for i in range(0, BLOCK // 2, size):
            pieces += [zeros, x[i : i + size]]
        return jnp.concatenate(pieces, axis=0)

    inverse = [eye - pick(x, 1) for x in lower]
    size = 2
    while size < BLOCK:
        split = [parts(x) for x in inverse]
        if size < 8:
            inner = [prod(pick(x, size), p) for x, p in zip(lower, split)]
            inverse = [t - prod(p, y) for t, p, y in zip(inverse, split, inner)]
        else:
            inner = [prod(second(pick(x, size), size), p) for x, p in zip(lower, split)]
            change = [prod(second(t, size), spread(y, size)) for t, y in zip(inverse, inner)]
            inverse = [t - spread(y, size) for t, y in zip(inverse, change)]
        size *= 2
    for h in range(group):
        t_ref[h, 0] = inverse[h]
    crows = [crow_ref[h] for h in range(group)]
    weights = [
        prod(t * (jnp.exp(c) * s[2]), k) for t, c, s, k in zip(inverse, crows, scales, keys)
    ]
    initial = each(prod, inverse, values)
    ends = [d[2] * s[1] for d, s in zip(decay, scales)]
    both = [
        prod(k, 2.0 * e * jnp.concatenate([w, u], axis=1), 0, 0)
        for k, e, w, u in zip(keys, ends, weights, initial)
    ]
    for h in range(group):
        w_ref[h, 0] = weights[h]
        u_ref[h, 0] = initial[h]
        a_ref[h, 0] = decay[h][3] * eye - both[h][:, :BLOCK]
        b_ref[h, 0] = both[h][:, BLOCK:]


def chain_kernel(
    q_ref, k_ref, g_ref, crow_ref, ccol_ref, inv_ref, gain_ref, gcol_ref, w_ref, a_ref, b_ref,
    inner_ref, c_ref, pre_ref, map_ref, adj_ref,
):
    group = crow_ref.shape[0]
    row, column = slots()

    @pl.when(pl.program_id(1) == 0)
    def _():
        eye = jnp.where(row == column, 1.0, 0.0)
        for h in range(group):
            map_ref[h, :, :BLOCK] = eye
            map_ref[h, :, BLOCK:] = jnp.zeros((BLOCK, BLOCK), jnp.float32)
            adj_ref[h] = jnp.zeros((BLOCK, BLOCK), jnp.float32)

    queries = lanes(q_ref, group)
    keys = lanes(k_ref, group)
    grads = lanes(g_ref, group)
    gains = lanes(gain_ref, group)
    inv = inv_ref[...]
    scales = key_scales(keys)
    decay = decays(crow_ref, ccol_ref, group)
    mixing = [
        prod(q, k.astype(jnp.float32) * gs, 1, 1) * (d[0] * inv * s[2])
        for q, k, gs, d, s in zip(queries, keys, gains, decay, scales)
    ]
    inner = [prod(m, g, 0, 0) for m, g in zip(mixing, grads)]
    direct = [
        gcol_ref[h] * prod(queries[h], (decay[h][1] * inv) * grads[h].astype(jnp.float32), 0, 0)
        for h in range(group)
    ]
    adjoint = [direct[h] - prod(w_ref[h, 0], inner[h], 0, 0) for h in range(group)]
    for h in range(group):
        before = map_ref[h]
        pre_ref[h, 0] = before
        inner_ref[h, 0] = inner[h]
        c_ref[h, 0] = adjoint[h]
        adj_ref[h] += prod(before[:, :BLOCK], adjoint[h], 0, 0)
        after = prod(a_ref[h, 0], before)
        map_ref[h, :, :BLOCK] = after[:, :BLOCK]
        map_ref[h, :, BLOCK:] = after[:, BLOCK:] + b_ref[h, 0]


def grads_kernel(
    count, full,
    q_ref, k_ref, g_ref, crow_ref, ccol_ref, inv_ref, gain_ref,
    t_ref, w_ref, u_ref, a_ref, c_ref, inner_ref, pre_ref, in_ref, out_ref,
    inv_cols, dq_hbm, dk_hbm, dv_hbm,
    carry_ref, scaled, query, grad, dkeys, dvalues, corr, held,
    corr_send, corr_recv, query_send, query_recv, send, receive, own_sem,
):
    group = crow_ref.shape[0]
    heads = range(group)
    row, column = slots()
    turn, step = pl.program_id(0), pl.program_id(1)
    turns, blocks, span_width = scaled.shape[0], corr.shape[0], group * BLOCK
    rows = scaled.shape[1]
    own = rows // count
    width = turns * span_width
    me = lax.axis_index("head")
    block = blocks - 1 - step
    place = pl.ds(pl.multiple_of(block * BLOCK, BLOCK), BLOCK)

    @pl.when(step == 0)
    def _():
        carry_ref[...] = out_ref[...]

    @pl.when((step == 0) & (turn == 0))
    def _():
        greet("head", count)
        corr[...] = jnp.zeros_like(corr)

    queries = lanes(q_ref, group)
    keys = lanes(k_ref, group)
    grads = lanes(g_ref, group)
    gains = lanes(gain_ref, group)
    inv = inv_ref[...]
    scales = key_scales(keys)
    decay = decays(crow_ref, ccol_ref, group)
    start = [
        parts(prod(pre_ref[h, 0, :, :BLOCK], in_ref[h]) + pre_ref[h, 0, :, BLOCK:]) for h in heads
    ]
    end = [parts(carry_ref[h]) for h in heads]
    fresh = [parts(u_ref[h, 0] - prod(w_ref[h, 0], start[h])) for h in heads]
    dfresh = [
        inner_ref[h, 0] + (2.0 * decay[h][2] * scales[h][1]) * prod(keys[h], end[h]) for h in heads
    ]
    for h in heads:
        carry_ref[h] = prod(a_ref[h, 0], end[h], 0, 0) + c_ref[h, 0]
    target = [prod(t_ref[h, 0], dfresh[h], 0, 0) for h in heads]
    tparts = [parts(x) for x in target]
    spread = [decay[h][0] * prod(grads[h], fresh[h], 1, 1) for h in heads]
    pairs = [
        jnp.where(row > column, decay[h][0] * prod(tparts[h], fresh[h], 1, 1), 0.0) for h in heads
    ]
    dquery = [
        decay[h][1] * prod(grads[h], start[h], 1, 1) + prod(spread[h] * scales[h][2], keys[h])
        for h in heads
    ]
    dkey = [
        2.0 * decay[h][2] * prod(fresh[h], end[h], 1, 1)
        - decay[h][1] * prod(tparts[h], start[h], 1, 1)
        for h in heads
    ]
    dkey = [
        dkey[h] - prod((pairs[h] + pairs[h].T) * scales[h][2], keys[h]) for h in heads
    ]
    dkey = [
        dkey[h] + gains[h] * prod(spread[h] * inv, queries[h], 0, 0) for h in heads
    ]
    total = jnp.zeros((BLOCK, 1), jnp.float32)
    query[turn, place, :] = q_ref[...]
    for h in heads:
        span = slice(h * BLOCK, (h + 1) * BLOCK)
        gradient = dquery[h] * gains[h]
        scaled[turn, place, span] = gradient
        total += jnp.sum(gradient * (queries[h].astype(jnp.float32) * inv), axis=1, keepdims=True)
        dvalues[turn, place, span] = target[h].astype(jnp.bfloat16)
        scale = scales[h][1]
        unit = keys[h].astype(jnp.float32) * scale
        along = jnp.sum(unit * dkey[h], axis=1, keepdims=True)
        dkeys[turn, place, span] = (scale * (dkey[h] - unit * along)).astype(jnp.bfloat16)
    corr[pl.ds(block, 1), :] += jnp.sum(jnp.where(row == column, total, 0.0), axis=0, keepdims=True)

    def owned(index):
        return pl.ds(pl.multiple_of(index * own, own), own)

    def columns(g):
        return pl.ds(pl.multiple_of(me * width + g * span_width, span_width), span_width)

    def moves(source, target, g, out_sem, in_sem, kept_sem):
        kept = pltpu.make_async_copy(
            source.at[g, owned(me)], target.at[:, columns(g)], kept_sem
        )
        sent = [
            remote(
                source.at[g, owned(lax.rem(me + k, count))],
                target.at[:, columns(g)],
                out_sem.at[g, k],
                in_sem.at[g, k],
                "head",
                lax.rem(me + k, count),
            )
            for k in range(1, count)
        ]
        return [kept] + sent

    def key_moves(g):
        return moves(dkeys, dk_hbm, g, send.at[0], receive.at[0], own_sem.at[0, g])

    def value_moves(g):
        return moves(dvalues, dv_hbm, g, send.at[1], receive.at[1], own_sem.at[1, g])

    def query_moves(g):
        return moves(grad, dq_hbm, g, query_send, query_recv, own_sem.at[2, g])

    @pl.when((step == blocks - 1) & (turn < turns - 1))
    def _():
        for pair in zip(key_moves(turn), value_moves(turn)):
            for copy in pair:
                copy.start()

    @pl.when((step == blocks - 1) & (turn == turns - 1))
    def _():
        shares = share_rows(count, corr, held, corr_send, corr_recv)
        for pair in zip(key_moves(turns - 1), value_moves(turns - 1)):
            for copy in pair:
                copy.start()
        for copy in shares:
            copy.wait()
        summed = corr[...]
        for k in range(1, count):
            summed += held[k]
        means = (summed / full).T
        for g in range(turns):
            for b in range(blocks):
                part = slice(b * BLOCK, (b + 1) * BLOCK)
                inverse = inv_cols[:, b : b + 1]
                normed = query[g, part, :].astype(jnp.float32) * inverse
                grad[g, part, :] = (
                    inverse * (scaled[g, part, :] - normed * means[:, b : b + 1])
                ).astype(jnp.bfloat16)
            for copy in query_moves(g):
                copy.start()
        for g in range(turns):
            for copy in key_moves(g) + value_moves(g) + query_moves(g):
                copy.wait()


def greet(axis, count):
    me = lax.axis_index(axis)
    barrier = pltpu.get_barrier_semaphore()
    for offset in range(1, count):
        pl.semaphore_signal(
            barrier,
            inc=1,
            device_id={axis: lax.rem(me + offset, count)},
            device_id_type=pl.DeviceIdType.MESH,
        )
    pl.semaphore_wait(barrier, count - 1)


def remote(source, target, send, receive, axis, index):
    return pltpu.make_async_remote_copy(
        src_ref=source,
        dst_ref=target,
        send_sem=send,
        recv_sem=receive,
        device_id={axis: index},
        device_id_type=pl.DeviceIdType.MESH,
    )


def share_rows(count, mine_ref, held_ref, send, receive):
    me = lax.axis_index("head")
    copies = [
        remote(
            mine_ref, held_ref.at[k], send.at[k], receive.at[k], "head", lax.rem(me + k, count)
        )
        for k in range(1, count)
    ]
    for copy in copies:
        copy.start()
    return copies


def total_kernel(count, mine_ref, total_ref, held_ref, send, receive):
    greet("head", count)
    copies = share_rows(count, mine_ref, held_ref, send, receive)
    for copy in copies:
        copy.wait()
    total = mine_ref[...]
    for k in range(1, count):
        total += held_ref[k]
    total_ref[...] = total


def states_kernel(
    count, map_ref, adj_ref, in_ref, out_ref,
    fsend, frecv, bsend, brecv, fsend_sem, frecv_sem, bsend_sem, brecv_sem,
):
    heads = adj_ref.shape[0]
    me = lax.axis_index("seq")
    first, last = me == 0, me == count - 1
    barrier = pltpu.get_barrier_semaphore()
    before, after = jnp.maximum(me - 1, 0), jnp.minimum(me + 1, count - 1)
    mesh_id = pl.DeviceIdType.MESH

    @pl.when(jnp.logical_not(first))
    def _():
        pl.semaphore_signal(barrier, inc=1, device_id={"seq": before}, device_id_type=mesh_id)

    @pl.when(jnp.logical_not(last))
    def _():
        pl.semaphore_signal(barrier, inc=1, device_id={"seq": after}, device_id_type=mesh_id)

    @pl.when(first | last)
    def _():
        pl.semaphore_wait(barrier, 1)

    @pl.when(jnp.logical_not(first | last))
    def _():
        pl.semaphore_wait(barrier, 2)

    def forward(h):
        return remote(
            fsend.at[h], frecv.at[h], fsend_sem.at[h], frecv_sem.at[h], "seq", after
        )

    def backward(h):
        return remote(
            bsend.at[h], brecv.at[h], bsend_sem.at[h], brecv_sem.at[h], "seq", before
        )

    def run(h, start, end, copy, recv, send, result, step):
        @pl.when(start)
        def _():
            result[h] = jnp.zeros_like(result[h])
            send[h] = step(h, None)

        @pl.when(jnp.logical_not(start))
        def _():
            copy(h).wait_recv()
            result[h] = recv[h]

            @pl.when(jnp.logical_not(end))
            def _():
                send[h] = step(h, recv[h])

        @pl.when(jnp.logical_not(end))
        def _():
            copy(h).start()

    def forward_step(h, state):
        offset = map_ref[h, :, BLOCK:]
        return offset if state is None else prod(map_ref[h, :, :BLOCK], state) + offset

    def backward_step(h, state):
        offset = adj_ref[h]
        return offset if state is None else prod(map_ref[h, :, :BLOCK], state, 0, 0) + offset

    def turn(t, _):
        h = t - me

        @pl.when((h >= 0) & (h < heads))
        def _():
            run(h, first, last, forward, frecv, fsend, in_ref, forward_step)

        k = t - (count - 1 - me)

        @pl.when((k >= 0) & (k < heads))
        def _():
            run(k, last, first, backward, brecv, bsend, out_ref, backward_step)

        return 0

    lax.fori_loop(0, heads + count - 1, turn, 0)

    @pl.when(jnp.logical_not(last))
    def _():
        for h in range(heads):
            forward(h).wait_send()

    @pl.when(jnp.logical_not(first))
    def _():
        for h in range(heads):
            backward(h).wait_send()


def per_device(query_raw, key_raw, value_raw, query_gain, log_decay, out_grad):
    rows, width = query_raw.shape
    heads = log_decay.shape[0]
    size = width // heads
    blocks = rows // BLOCK
    full = width * lax.axis_size("head")
    f32 = jnp.float32

    raw_query = query_raw.astype(f32)
    count = lax.axis_size("head")
    turns = lax.axis_size("seq")
    dma = pltpu.SemaphoreType.DMA
    in_vmem = pl.BlockSpec(memory_space=pltpu.VMEM)
    anywhere = pl.BlockSpec(memory_space=pl.ANY)
    row_shape = jax.ShapeDtypeStruct((blocks, BLOCK), f32)
    squares = pl.pallas_call(
        functools.partial(total_kernel, count),
        in_specs=[in_vmem],
        out_specs=in_vmem,
        out_shape=row_shape,
        scratch_shapes=[pltpu.VMEM((count, blocks, BLOCK), f32), dma((count,)), dma((count,))],
        compiler_params=pltpu.CompilerParams(collective_id=0, has_side_effects=True),
        name="token_squares",
    )(jnp.sum((raw_query * raw_query).reshape(blocks, BLOCK, width), axis=2))
    inv_rows = lax.rsqrt(squares / full + epsilon)
    inv = inv_rows.reshape(rows, 1)
    gain = query_gain * size ** (-0.5)
    gain_row = gain[None, :]
    gain_col = gain.reshape(heads, size, 1)
    cumul = jnp.cumsum(log_decay.reshape(heads, blocks, BLOCK), axis=2).reshape(heads, rows)
    crow = cumul[:, None, :]

    def columns_of(group):
        return cumul.reshape(heads // group, group, rows).transpose(0, 2, 1)

    def specs(group, order):
        return dict(
            raw=pl.BlockSpec((BLOCK, group * size), lambda g, b: (order(b), g)),
            crow=pl.BlockSpec((group, 1, BLOCK), lambda g, b: (g, 0, order(b))),
            ccol=pl.BlockSpec((1, BLOCK, group), lambda g, b: (g, order(b), 0)),
            inv=pl.BlockSpec((BLOCK, 1), lambda g, b: (order(b), 0)),
            gain=pl.BlockSpec((1, group * size), lambda g, b: (0, g)),
            gcol=pl.BlockSpec((group, size, 1), lambda g, b: (g, 0, 0)),
            mat=pl.BlockSpec((group, 1, size, size), lambda g, b: (g, order(b), 0, 0)),
            pre=pl.BlockSpec((group, 1, size, 2 * size), lambda g, b: (g, order(b), 0, 0)),
            head=pl.BlockSpec((group, size, size), lambda g, b: (g, 0, 0)),
            map=pl.BlockSpec((group, size, 2 * size), lambda g, b: (g, 0, 0)),
            corr=pl.BlockSpec((1, BLOCK, 1), lambda g, b: (g, order(b), 0)),
        )

    mat = jax.ShapeDtypeStruct((heads, blocks, size, size), f32)
    pre = jax.ShapeDtypeStruct((heads, blocks, size, 2 * size), f32)
    params = pltpu.CompilerParams(
        dimension_semantics=("arbitrary", "arbitrary"), vmem_limit_bytes=VMEM
    )

    def cost(passes):
        flops = 2 * passes * BLOCK**3 * heads * blocks
        return pl.CostEstimate(flops=flops, bytes_accessed=24 * 2**20, transcendentals=0)

    group = math.gcd(heads, WIDE)
    grid = (heads // group, blocks)
    ccol = columns_of(group)
    s = specs(group, lambda b: b)
    inverse, weight, initial, trans, offset = pl.pallas_call(
        maps_kernel,
        grid=grid,
        in_specs=[s["raw"], s["raw"], s["crow"], s["ccol"]],
        out_specs=[s["mat"]] * 5,
        out_shape=[mat] * 5,
        compiler_params=params,
        cost_estimate=cost(160),
        name="block_maps",
    )(key_raw, value_raw, crow, ccol)
    inner, adjoint, prefix, device_map, device_adjoint = pl.pallas_call(
        chain_kernel,
        grid=grid,
        in_specs=[s["raw"]] * 3
        + [s["crow"], s["ccol"], s["inv"], s["gain"], s["gcol"]]
        + [s["mat"]] * 3,
        out_specs=[s["mat"], s["mat"], s["pre"], s["map"], s["head"]],
        out_shape=[
            mat,
            mat,
            pre,
            jax.ShapeDtypeStruct((heads, size, 2 * size), f32),
            jax.ShapeDtypeStruct((heads, size, size), f32),
        ],
        compiler_params=params,
        cost_estimate=cost(80),
        name="device_maps",
    )(
        query_raw, key_raw, out_grad, crow, ccol, inv, gain_row, gain_col, weight, trans, offset
    )

    state = jax.ShapeDtypeStruct((heads, size, size), f32)
    incoming, outgoing = pl.pallas_call(
        functools.partial(states_kernel, turns),
        in_specs=[in_vmem, in_vmem],
        out_specs=[in_vmem, in_vmem],
        out_shape=[state, state],
        scratch_shapes=[pltpu.VMEM((heads, size, size), f32)] * 4 + [dma((heads,))] * 4,
        compiler_params=pltpu.CompilerParams(
            collective_id=1, has_side_effects=True, vmem_limit_bytes=VMEM
        ),
        name="device_states",
    )(device_map, device_adjoint)

    group = math.gcd(heads, GROUP)
    groups = heads // group
    grid = (groups, blocks)
    ccol = columns_of(group)
    s = specs(group, lambda b: blocks - 1 - b)
    owned = jax.ShapeDtypeStruct((rows // count, full), jnp.bfloat16)
    span = group * size
    half = pltpu.VMEM((groups, rows, span), jnp.bfloat16)
    return pl.pallas_call(
        functools.partial(grads_kernel, count, full),
        grid=grid,
        in_specs=[s["raw"]] * 3
        + [s["crow"], s["ccol"], s["inv"], s["gain"]]
        + [s["mat"]] * 6
        + [s["pre"], s["head"], s["head"], pl.BlockSpec((BLOCK, blocks), lambda g, b: (0, 0))],
        out_specs=[anywhere] * 3,
        out_shape=[owned] * 3,
        scratch_shapes=[
            pltpu.VMEM((group, size, size), f32),
            pltpu.VMEM((groups, rows, span), f32),
            half,
            half,
            half,
            half,
            pltpu.VMEM((blocks, BLOCK), f32),
            pltpu.VMEM((count, blocks, BLOCK), f32),
            dma((count,)),
            dma((count,)),
            dma((groups, count)),
            dma((groups, count)),
            dma((2, groups, count)),
            dma((2, groups, count)),
            dma((3, groups)),
        ],
        compiler_params=pltpu.CompilerParams(
            dimension_semantics=("arbitrary", "arbitrary"),
            collective_id=2,
            has_side_effects=True,
            vmem_limit_bytes=VMEM,
        ),
        name="block_grads",
    )(
        query_raw, key_raw, out_grad, crow, ccol, inv, gain_row,
        inverse, weight, initial, trans, adjoint, inner, prefix, incoming, outgoing,
        inv_rows.T,
    )


def solution(mesh):
    in_specs = (
        P("seq", "head"),
        P("seq", "head"),
        P("seq", "head"),
        P("head"),
        P("head", "seq"),
        P("seq", "head"),
    )
    out_specs = (P(("seq", "head"), None), P(("seq", "head"), None), P(("seq", "head"), None))
    return jax.shard_map(
        per_device, mesh=mesh, in_specs=in_specs, out_specs=out_specs, check_vma=False
    )
```
